32 devices in a mesh: dp: 32 (over z, y, x, core).
Axes of the slice: x: 2, y: 2, z: 4, core: 2. Of those that a mesh axis runs over, the one named last changes fastest.
Arguments:
- tokens: bfloat16 [2, 8192, 1024], P(None, 'dp'), may hold values from -6 to 6
- cotangent: bfloat16 [2, 8192, 1024], P(None, 'dp'), may hold values from -6 to 6
- segment_ids: int32 [2, 32, 256], P(None, 'dp'), may hold values from 0 to 3, never falling along the last dimension, each value on 1 to 128 neighbouring positions
- norm_gain: bfloat16 [1024], P('dp'), may hold values from 0.5 to 1.5
- w_query: bfloat16 [1024, 512], P('dp'), may hold values from -0.1875 to 0.1875
- w_key: bfloat16 [1024, 128], P('dp'), may hold values from -0.1875 to 0.1875
- w_value: bfloat16 [1024, 128], P('dp'), may hold values from -0.1875 to 0.1875
- w_attn_out: bfloat16 [512, 1024], P('dp'), may hold values from -1 to 1
- w_ssm_z: bfloat16 [1024, 1536], P('dp'), may hold values from -0.1875 to 0.1875
- w_ssm_x: bfloat16 [1024, 1536], P('dp'), may hold values from -0.1875 to 0.1875
- w_bc: bfloat16 [1024, 256], P('dp'), may hold values from -0.1875 to 0.1875
- w_delta: bfloat16 [1024, 24], P('dp'), may hold values from -0.1875 to 0.1875
- conv_weight: bfloat16 [1792, 4], P('dp'), may hold values from -3 to 3
- conv_bias: bfloat16 [1792], P('dp'), may hold values from -3 to 3
- ssm_gain: bfloat16 [1536], P('dp'), may hold values from 0.5 to 1.5
- w_ssm_out: bfloat16 [1536, 1024], P('dp'), may hold values from -0.15625 to 0.15625
- norm2_gain: bfloat16 [1024], P('dp'), may hold values from 0.5 to 1.5
- w_gate: bfloat16 [1024, 2048], P('dp'), may hold values from -0.1875 to 0.1875
- w_up: bfloat16 [1024, 2048], P('dp'), may hold values from -0.1875 to 0.1875
- w_down: bfloat16 [2048, 1024], P('dp'), may hold values from -0.125 to 0.125
- delta_bias: float32 [24], replicated, may hold values from -4 to -1
- decay_log: float32 [24], replicated, may hold values from -2 to 1
- skip_gain: float32 [24], replicated, may hold values from 0.5 to 1.5
Outputs:
- outputs: bfloat16 [2, 8192, 1024], P(None, 'dp')
- input_grad: float32 [2, 8192, 1024], P(None, 'dp')
- grad_norm_gain: float32 [1024], P('dp')
- grad_query: float32 [1024, 512], P('dp')
- grad_key: float32 [1024, 128], P('dp')
- grad_value: float32 [1024, 128], P('dp')
- grad_attn_out: float32 [512, 1024], P('dp')
- grad_ssm_z: float32 [1024, 1536], P('dp')
- grad_ssm_x: float32 [1024, 1536], P('dp')
- grad_bc: float32 [1024, 256], P('dp')
- grad_delta: float32 [1024, 24], P('dp')
- grad_conv_weight: float32 [1792, 4], P('dp')
- grad_conv_bias: float32 [1792], P('dp')
- grad_ssm_gain: float32 [1536], P('dp')
- grad_ssm_out: float32 [1536, 1024], P('dp')
- grad_norm2_gain: float32 [1024], P('dp')
- grad_gate: float32 [1024, 2048], P('dp')
- grad_up: float32 [1024, 2048], P('dp')
- grad_down: float32 [2048, 1024], P('dp')
- grad_delta_bias: float32 [24], replicated
- grad_decay_log: float32 [24], replicated
- grad_skip_gain: float32 [24], replicated
The draws below stay inside these ranges and needn't reach their ends.
Inputs may be any that keep to these rules, and one draw needn't show every extreme that they name: `segment_ids`: within each row of 256 tokens of one device and micro-batch the ids never fall; each sequence has 1 to 128 tokens and one of them exactly 128.
All inputs are finite; a program needn't handle non-finite values.
Results may differ from the reference program's by a relative error of at most 0.017.
Values may be sent and summed in bfloat16 or wider, within the bound.
A program may use at most 256 MiB of HBM per device.

```python
import math
import jax
import jax.numpy as jnp
import numpy as np
from jax import lax

D = 1024
Q_HEADS = 8
KV_HEADS = 2
HEAD_DIM = 64
SSM_HEADS = 24
STATE = 128
KCONV = 4
FF = 2048
MICRO = 2
TOK_MB = 256
SEGS = 4
SEG_MOST = 128
SSM_WIDTH = 1536
CHAN = 1792
TOKENS = 8192
N_DP = 32


def level_of(own_key, extent, shards, low, high):
    factor_of, own = 1.0, jax.random.fold_in(own_key, 6)
    for dim, blocks in shards:
        heights = jnp.exp(jax.random.uniform(jax.random.fold_in(own, dim), (blocks,), jnp.float32, low / len(shards), high / len(shards)))
        factor_of = factor_of * jnp.repeat(heights, extent[dim] // blocks).reshape([-1 if axis == dim else 1 for axis in range(len(extent))])
    return factor_of


def length_profile(count, total, most, skew):
    weights = [(1 << 20) // math.isqrt(grade ** skew) + 1 for grade in range(2, count + 1)]
    surplus, holding = total - most - (count - 1), [1] * (count - 1)
    while surplus > 0:
        candidates = [i for i in range(count - 1) if holding[i] < most]
        pool, left = sum([weights[i] for i in candidates]), surplus
        for i in candidates:
            more = min(most - holding[i], max(1, left * weights[i] // pool), surplus)
            holding[i] = holding[i] + more
            surplus = surplus - more
    return np.array([most] + holding)


def uneven(own_key, count, total, limit, skew):
    if count == 2:
        one = jax.random.randint(own_key, (), max(1, total - limit), min(limit, total - 1) + 1)
        return jnp.stack([one, total - one])
    lengths = jnp.asarray(length_profile(count, total, limit, skew), jnp.int32)
    couples = (count - 1) // 2
    giver, sink = lengths[1:1 + 2 * couples:2], lengths[2:2 + 2 * couples:2]
    margin = jnp.minimum(giver - 1, limit - sink)
    shifted = jax.random.randint(jax.random.fold_in(own_key, 1), (couples,), 0, 1 << 20) % (margin + 1)
    lengths = lengths.at[1:1 + 2 * couples:2].set(giver - shifted).at[2:2 + 2 * couples:2].set(sink + shifted)
    return lengths[jax.random.permutation(jax.random.fold_in(own_key, 2), count)]


def bell_draw(key, extent, spread, bound, shards=(), held_as=jnp.bfloat16):
    values = jax.random.normal(key, extent, jnp.float32) * spread
    if len(shards) > 0:
        values = level_of(key, extent, shards, -0.22, 0.18) * values
    return jnp.clip(values, min=-bound, max=bound).astype(held_as)


def setup_inputs(seed: int = 0) -> dict:
    streams_of = jax.random.split(jax.random.key(seed), 24)
    return {
        "tokens": bell_draw(streams_of[0], (MICRO, TOKENS, D), 1.0, 6.0, ((1, 32),)),
        "cotangent": bell_draw(streams_of[1], (MICRO, TOKENS, D), 1.0, 6.0, ((1, 32),)),
        "segment_ids": jax.vmap(lambda own: jnp.searchsorted(jnp.cumsum(uneven(own, SEGS, TOK_MB, SEG_MOST, 2)), jnp.arange(TOK_MB), side="right"))(jax.random.split(streams_of[2], MICRO * N_DP)).reshape((MICRO, N_DP, TOK_MB)).astype(jnp.int32),
        "norm_gain": jnp.clip(1.0 + 0.1 * jax.random.normal(streams_of[3], (D,), jnp.float32), 0.5, 1.5).astype(jnp.bfloat16),
        "w_query": bell_draw(streams_of[4], (D, Q_HEADS * HEAD_DIM), D ** -0.5, 0.1875, ((0, 32),)),
        "w_key": bell_draw(streams_of[5], (D, KV_HEADS * HEAD_DIM), D ** -0.5, 0.1875, ((0, 32),)),
        "w_value": bell_draw(streams_of[6], (D, KV_HEADS * HEAD_DIM), D ** -0.5, 0.1875, ((0, 32),)),
        "w_attn_out": bell_draw(streams_of[7], (Q_HEADS * HEAD_DIM, D), (Q_HEADS * HEAD_DIM // 16) ** -0.5, 1.0, ((0, 32),)),
        "w_ssm_z": bell_draw(streams_of[8], (D, SSM_WIDTH), D ** -0.5, 0.1875, ((0, 32),)),
        "w_ssm_x": bell_draw(streams_of[9], (D, SSM_WIDTH), D ** -0.5, 0.1875, ((0, 32),)),
        "w_bc": bell_draw(streams_of[10], (D, 2 * STATE), D ** -0.5, 0.1875, ((0, 32),)),
        "w_delta": bell_draw(streams_of[11], (D, SSM_HEADS), D ** -0.5, 0.1875, ((0, 32),)),
        "conv_weight": bell_draw(streams_of[12], (CHAN, KCONV), KCONV ** -0.5, 3.0, ((0, 32),)),
        "conv_bias": bell_draw(streams_of[13], (CHAN,), 0.5, 3.0, ((0, 32),)),
        "ssm_gain": jnp.clip(1.0 + 0.1 * jax.random.normal(streams_of[14], (SSM_WIDTH,), jnp.float32), 0.5, 1.5).astype(jnp.bfloat16),
        "w_ssm_out": bell_draw(streams_of[15], (SSM_WIDTH, D), SSM_WIDTH ** -0.5, 0.15625, ((0, 32),)),
        "norm2_gain": jnp.clip(1.0 + 0.1 * jax.random.normal(streams_of[16], (D,), jnp.float32), 0.5, 1.5).astype(jnp.bfloat16),
        "w_gate": bell_draw(streams_of[17], (D, FF), D ** -0.5, 0.1875, ((0, 32),)),
        "w_up": bell_draw(streams_of[18], (D, FF), D ** -0.5, 0.1875, ((0, 32),)),
        "w_down": bell_draw(streams_of[19], (FF, D), FF ** -0.5, 0.125, ((0, 32),)),
        "delta_bias": jnp.clip(jax.random.uniform(streams_of[20], (SSM_HEADS,), jnp.float32, -4.0, -1.0), -4.0, -1.0),
        "decay_log": jnp.clip(jax.random.uniform(streams_of[21], (SSM_HEADS,), jnp.float32, -2.0, 1.0), -2.0, 1.0),
        "skip_gain": jnp.clip(jax.random.uniform(streams_of[22], (SSM_HEADS,), jnp.float32, 0.5, 1.5), 0.5, 1.5),
    }


EPS = 1e-05
NEG = -1e+30
HIGH = lax.Precision.HIGHEST

@jax.custom_vjp
def low(v):
    return lax.optimization_barrier(v.astype(jnp.bfloat16)).astype(jnp.float32)

@jax.custom_vjp
def low_back(v):
    return v

def low_keep(v):
    return (low(v), None)

def low_pass(kept, grad):
    return (grad,)

def back_keep(v):
    return (v, None)

def back_low(kept, grad):
    return (low(grad),)
low.defvjp(low_keep, low_pass)
low_back.defvjp(back_keep, back_low)

def product(left, right):
    return jnp.dot(left, right, precision=HIGH, preferred_element_type=jnp.float32)

def rms_norm(value, gain):
    return value * lax.rsqrt(lax.optimization_barrier(jnp.mean(value * value, axis=-1, keepdims=True)) + EPS) * gain

def causal_mask(segs):
    places = jnp.arange(segs.shape[0])
    return (places[:, None] >= places[None, :]) & (segs[:, None] == segs[None, :])

def conv_masks(segs):
    masks = []
    for shift_by in range(1, KCONV):
        earlier = jnp.concatenate([jnp.full((shift_by,), -1, jnp.int32), segs[:-shift_by].astype(jnp.int32)])
        masks.append((segs.astype(jnp.int32) == earlier).astype(jnp.float32)[:, None])
    return masks

def shift_down(value, shift_by):
    return jnp.concatenate([jnp.zeros((shift_by, value.shape[1]), value.dtype), value[:-shift_by]], axis=0)

def conv_forward(conv_in, conv_weight, conv_bias, masks):
    result = conv_in * conv_weight[:, KCONV - 1]
    for shift_by in range(1, KCONV):
        result = result + masks[shift_by - 1] * shift_down(conv_in, shift_by) * conv_weight[:, KCONV - 1 - shift_by]
    return result + conv_bias

def decay(column, allowed):
    diff = column[:, None] - column[None, :]
    return jnp.where(allowed, jnp.exp(jnp.where(allowed, diff, 0.0)), 0.0)

def layer(inputs, params, heads, segs):
    norm_gain, w_query, w_key, w_value, w_attn_out, w_ssm_z, w_ssm_x, w_bc, w_delta, conv_weight, conv_bias, ssm_gain, w_ssm_out, norm2_gain, w_gate, w_up, w_down = params
    delta_bias, decay_log, skip_gain = heads
    length = inputs.shape[0]
    group = Q_HEADS // KV_HEADS
    allowed = causal_mask(segs)
    normed = low(low_back(rms_norm(inputs, norm_gain)))
    queries = low(low_back(product(normed, w_query))).reshape(length, Q_HEADS, HEAD_DIM).transpose(1, 0, 2)
    keys = low(low_back(product(normed, w_key))).reshape(length, KV_HEADS, HEAD_DIM).transpose(1, 0, 2)
    values = low(low_back(product(normed, w_value))).reshape(length, KV_HEADS, HEAD_DIM).transpose(1, 0, 2)
    keys = jnp.repeat(keys, group, axis=0)
    values = jnp.repeat(values, group, axis=0)
    scores = low_back(jnp.einsum('hid,hjd->hij', queries, keys, precision=HIGH) * HEAD_DIM ** (-0.5))
    scores = jnp.where(allowed[None], scores, NEG)
    expo = jnp.exp(scores - lax.optimization_barrier(jnp.max(scores, axis=-1, keepdims=True)))
    probs = low(expo / lax.optimization_barrier(jnp.sum(expo, axis=-1, keepdims=True)))
    attended = jnp.einsum('hij,hjd->ihd', probs, values, precision=HIGH).reshape(length, Q_HEADS * HEAD_DIM)
    attended = low(low_back(attended))
    attn_part = product(attended, w_attn_out)
    gate_z = low_back(product(normed, w_ssm_z))
    inner_x = low_back(product(normed, w_ssm_x))
    inner_bc = low_back(product(normed, w_bc))
    delta_raw = low_back(product(normed, w_delta))
    conv_in = jnp.concatenate([inner_x, inner_bc], axis=1)
    conv_out = jax.nn.silu(conv_forward(conv_in, conv_weight, conv_bias, conv_masks(segs)))
    width = SSM_HEADS * HEAD_DIM
    mixed_x = conv_out[:, :width].reshape(length, SSM_HEADS, HEAD_DIM)
    state_in = low(low_back(conv_out[:, width:width + STATE]))
    state_out = low(low_back(conv_out[:, width + STATE:]))
    delta = jax.nn.softplus(delta_raw + delta_bias)
    rates = -jnp.exp(decay_log)
    cumul = jnp.cumsum(delta * rates, axis=0)
    coupling = low_back(product(state_out, state_in.T))
    decays = jax.vmap(lambda column: decay(column, allowed))(cumul.T)
    ssd_weights = low(low_back(coupling[None] * decays))
    scaled_x = low(low_back(delta[:, :, None] * mixed_x))
    ssd = low_back(jnp.einsum('hij,jhd->ihd', ssd_weights, scaled_x, precision=HIGH))
    ssm_y = (ssd + skip_gain[None, :, None] * mixed_x).reshape(length, width)
    gated = ssm_y * jax.nn.silu(gate_z)
    ssm_part = product(low(rms_norm(gated, ssm_gain)), w_ssm_out)
    mixer = low_back(attn_part + ssm_part)
    resid = inputs + mixer
    normed2 = low(low_back(rms_norm(resid, norm2_gain)))
    gate_pre = low_back(product(normed2, w_gate))
    up_pre = low_back(product(normed2, w_up))
    hidden = low(jax.nn.silu(gate_pre) * up_pre)
    return resid + product(hidden, w_down)

def reference(tokens, cotangent, segment_ids, norm_gain, w_query, w_key, w_value, w_attn_out, w_ssm_z, w_ssm_x, w_bc, w_delta, conv_weight, conv_bias, ssm_gain, w_ssm_out, norm2_gain, w_gate, w_up, w_down, delta_bias, decay_log, skip_gain):
    params = tuple((item.astype(jnp.float32) for item in (norm_gain, w_query, w_key, w_value, w_attn_out, w_ssm_z, w_ssm_x, w_bc, w_delta, conv_weight, conv_bias, ssm_gain, w_ssm_out, norm2_gain, w_gate, w_up, w_down)))
    heads = (delta_bias.astype(jnp.float32), decay_log.astype(jnp.float32), skip_gain.astype(jnp.float32))
    rows_in = tokens.astype(jnp.float32).reshape(MICRO * N_DP, TOK_MB, D)
    rows_back = cotangent.astype(jnp.float32).reshape(MICRO * N_DP, TOK_MB, D)
    rows_seg = segment_ids.reshape(MICRO * N_DP, TOK_MB).astype(jnp.int32)
    zeros = jax.tree.map(jnp.zeros_like, (params, heads))

    def step(carry, row):
        row_in, row_back, row_seg = row
        result, pullback = jax.vjp(lambda first, second, third: layer(first, second, third, row_seg), row_in, params, heads)
        grad_in, grad_params, grad_heads = pullback(row_back)
        carry = jax.tree.map(jnp.add, carry, (grad_params, grad_heads))
        return (carry, (result.astype(jnp.bfloat16), grad_in))
    totals, (results, grads_in) = lax.scan(step, zeros, (rows_in, rows_back, rows_seg))
    return (results.reshape(MICRO, TOKENS, D), grads_in.reshape(MICRO, TOKENS, D), *totals[0], *totals[1])
```

```python
import jax
import jax.numpy as jnp
from jax import lax
from jax.sharding import PartitionSpec as P

Q_HEADS = 8
KV_HEADS = 2
HEAD_DIM = 64
SSM_HEADS = 24
STATE = 128
KCONV = 4


EPS = 1e-05
NEG = -1e30


def matmul(left, right):
    return jnp.dot(left, right, preferred_element_type=jnp.float32)


def left_product(left, right):
    return lax.dot_general(
        left, right, (((0,), (0,)), ((), ())), preferred_element_type=jnp.float32
    )


def right_product(left, right):
    return lax.dot_general(
        left, right, (((1,), (1,)), ((), ())), preferred_element_type=jnp.float32
    )


def to_low(value):
    return value.astype(jnp.bfloat16)


def norm_forward(value, gain):
    inverse = lax.rsqrt(jnp.mean(value * value, axis=-1, keepdims=True) + EPS)
    return (value * inverse * gain, inverse)


def norm_backward(value, inverse, gain, grad):
    scaled = grad * gain
    gain_grad = jnp.sum(grad * value * inverse, axis=0)
    value_grad = inverse * scaled - value * inverse**3 * jnp.mean(
        scaled * value, axis=-1, keepdims=True
    )
    return (value_grad, gain_grad)


def silu_slope(value):
    sigma = jax.nn.sigmoid(value)
    return sigma * (1.0 + value * (1.0 - sigma))


def shift_down(value, by):
    return jnp.pad(value, ((0, 0), (by, 0), (0, 0)))[:, : value.shape[1]]


def shift_up(value, by):
    return jnp.pad(value, ((0, 0), (0, by), (0, 0)))[:, by:]


def batched(equation, left, right):
    return jnp.einsum(equation, left, right, preferred_element_type=jnp.float32)


def pack_vectors(vectors, rows):
    flat = jnp.concatenate([vector.reshape(-1) for vector in vectors])
    wide = -(-flat.size // rows)
    return jnp.pad(flat, (0, rows * wide - flat.size)).reshape(rows, wide)


def per_device(
    tokens,
    cotangent,
    segment_ids,
    norm_gain,
    w_query,
    w_key,
    w_value,
    w_attn_out,
    w_ssm_z,
    w_ssm_x,
    w_bc,
    w_delta,
    conv_weight,
    conv_bias,
    ssm_gain,
    w_ssm_out,
    norm2_gain,
    w_gate,
    w_up,
    w_down,
    delta_bias,
    decay_log,
    skip_gain,
):
    f32 = jnp.float32
    count = lax.axis_size("dp")
    micro, length, model = tokens.shape
    total = micro * length
    rows = w_query.shape[0]
    group = Q_HEADS // KV_HEADS
    scale = HEAD_DIM ** (-0.5)
    width = SSM_HEADS * HEAD_DIM
    chan = width + 2 * STATE
    q_width, kv_width = Q_HEADS * HEAD_DIM, KV_HEADS * HEAD_DIM

    vectors = (norm_gain, conv_weight, conv_bias, ssm_gain, norm2_gain)
    small = pack_vectors(vectors, rows)
    main_width = q_width + 2 * kv_width + width + chan
    tail_width = -(-(SSM_HEADS + small.shape[1]) // 128) * 128
    spare = tail_width - SSM_HEADS - small.shape[1]
    own_in = jnp.concatenate(
        [
            w_query,
            w_key,
            w_value,
            w_ssm_z,
            w_ssm_x,
            w_bc,
            w_delta,
            small,
            jnp.zeros((rows, spare), small.dtype),
        ],
        axis=1,
    )
    w_in = lax.all_gather(own_in, "dp", axis=0, tiled=True)
    own_mix = jnp.concatenate([w_attn_out, w_ssm_out], axis=0)
    w_mix = lax.all_gather(own_mix, "dp", axis=0, tiled=True)
    w_ff = lax.all_gather(jnp.concatenate([w_gate, w_up], axis=1), "dp", axis=0, tiled=True)
    w_back = lax.all_gather(w_down, "dp", axis=0, tiled=True)
    packed = w_in[:, main_width + SSM_HEADS : main_width + SSM_HEADS + small.shape[1]]
    packed = packed.reshape(count, -1)
    gains = []
    offset = 0
    for vector in vectors:
        part = packed[:, offset : offset + vector.size]
        gains.append(part.reshape((count * vector.shape[0],) + vector.shape[1:]).astype(f32))
        offset += vector.size
    gain1, taps, bias, gain3, gain2 = gains
    attn_rows = w_attn_out.shape[0]
    w_mix = w_mix.reshape(count, own_mix.shape[0], model)
    w_attn = w_mix[:, :attn_rows].reshape(-1, model)
    w_ssm = w_mix[:, attn_rows:].reshape(-1, model)
    ff = w_gate.shape[1]

    segs = segment_ids[:, 0]
    places = jnp.arange(length)
    causal = places[:, None] >= places[None, :]
    allowed = causal[None] & (segs[:, :, None] == segs[:, None, :])
    masks = []
    for by in range(1, KCONV):
        earlier = jnp.pad(segs, ((0, 0), (by, 0)), constant_values=-1)[:, :length]
        masks.append((segs == earlier).astype(f32)[:, :, None])
    inputs = tokens.reshape(total, model).astype(f32)
    normed, inverse1 = norm_forward(inputs, gain1)
    normed_low = to_low(normed)
    projected = matmul(normed_low, w_in)
    cut = q_width
    queries = to_low(projected[:, :cut]).reshape(micro, length, KV_HEADS, group, HEAD_DIM)
    keys = to_low(projected[:, cut : cut + kv_width]).reshape(micro, length, KV_HEADS, HEAD_DIM)
    cut += kv_width
    values = to_low(projected[:, cut : cut + kv_width]).reshape(micro, length, KV_HEADS, HEAD_DIM)
    cut += kv_width
    gate_z = projected[:, cut : cut + width]
    cut += width
    conv_in = projected[:, cut : cut + chan].reshape(micro, length, chan)
    delta_raw = projected[:, main_width : main_width + SSM_HEADS].reshape(micro, length, SSM_HEADS)

    scores = batched("migkd,mjgd->mgkij", queries, keys) * scale
    scores = jnp.where(allowed[:, None, None], scores, NEG)
    expo = jnp.exp(scores - jnp.max(scores, axis=-1, keepdims=True))
    probs = expo / jnp.sum(expo, axis=-1, keepdims=True)
    probs_low = to_low(probs)
    attended = to_low(batched("mgkij,mjgd->migkd", probs_low, values).reshape(total, q_width))

    conv_pre = conv_in * taps[:, KCONV - 1] + bias
    for by in range(1, KCONV):
        conv_pre += masks[by - 1] * shift_down(conv_in, by) * taps[:, KCONV - 1 - by]
    conv_out = jax.nn.silu(conv_pre)
    mixed_x = conv_out[:, :, :width].reshape(micro, length, SSM_HEADS, HEAD_DIM)
    state_in = to_low(conv_out[:, :, width : width + STATE])
    state_out = to_low(conv_out[:, :, width + STATE :])
    delta = jax.nn.softplus(delta_raw + delta_bias)
    rates = -jnp.exp(decay_log)
    lower = causal.astype(f32)
    cumul = jnp.einsum("ij,mjh->mhi", lower, delta * rates, precision=lax.Precision.HIGHEST)
    coupling = batched("mis,mjs->mij", state_out, state_in)
    scaled_x = to_low(delta[..., None] * mixed_x).transpose(0, 2, 1, 3)
    diff = cumul[:, :, :, None] - cumul[:, :, None, :]
    near = allowed[:, None]
    decays = jnp.where(near, jnp.exp(jnp.where(near, diff, 0.0)), 0.0)
    ssd_weights = to_low(coupling[:, None] * decays)
    ssd = batched("mhij,mhjd->mhid", ssd_weights, scaled_x)
    ssm_y = (ssd.transpose(0, 2, 1, 3) + skip_gain[:, None] * mixed_x).reshape(total, width)
    gate_silu = jax.nn.silu(gate_z)
    gated = ssm_y * gate_silu
    ssm_normed, inverse3 = norm_forward(gated, gain3)
    ssm_low = to_low(ssm_normed)
    resid = inputs + (matmul(attended, w_attn) + matmul(ssm_low, w_ssm))
    normed2, inverse2 = norm_forward(resid, gain2)
    normed2_low = to_low(normed2)
    pre = matmul(normed2_low, w_ff)
    gate_pre, up_pre = pre[:, :ff], pre[:, ff:]
    gate_sigma = jax.nn.sigmoid(gate_pre)
    hidden = to_low(gate_pre * gate_sigma * up_pre)
    output = to_low(resid + matmul(hidden, w_back))

    upstream = cotangent.reshape(total, model)
    grad_back = to_low(left_product(hidden, upstream))
    owned_back = lax.psum_scatter(grad_back, "dp", scatter_dimension=0, tiled=True)
    hidden_grad = right_product(upstream, w_back)
    gate_grad = to_low(hidden_grad * up_pre * gate_sigma * (1.0 + gate_pre * (1.0 - gate_sigma)))
    up_grad = to_low(hidden_grad * gate_pre * gate_sigma)
    pre_grad = jnp.concatenate([gate_grad, up_grad], axis=1)
    grad_ff = to_low(left_product(normed2_low, pre_grad))
    owned_ff = lax.psum_scatter(grad_ff, "dp", scatter_dimension=0, tiled=True)
    normed2_grad = to_low(right_product(pre_grad, w_ff)).astype(f32)
    resid_part, gain2_grad = norm_backward(resid, inverse2, gain2, normed2_grad)
    resid_grad = upstream.astype(f32) + resid_part
    mixer_grad = to_low(resid_grad)
    grad_mix = jnp.concatenate(
        [
            to_low(left_product(attended, mixer_grad)).reshape(count, -1, model),
            to_low(left_product(ssm_low, mixer_grad)).reshape(count, -1, model),
        ],
        axis=1,
    ).reshape(-1, model)
    owned_mix = lax.psum_scatter(grad_mix, "dp", scatter_dimension=0, tiled=True)

    ssm_normed_grad = right_product(mixer_grad, w_ssm)
    gated_grad, gain3_grad = norm_backward(gated, inverse3, gain3, ssm_normed_grad)
    ssm_y_grad = (gated_grad * gate_silu).reshape(micro, length, SSM_HEADS, HEAD_DIM)
    gate_z_grad = to_low(gated_grad * ssm_y * silu_slope(gate_z))
    skip_grad = jnp.sum(ssm_y_grad * mixed_x, axis=(0, 1, 3))
    ssd_grad = to_low(ssm_y_grad).transpose(0, 2, 1, 3)
    scaled_grad = to_low(batched("mhij,mhid->mhjd", ssd_weights, ssd_grad))
    weights_grad = to_low(batched("mhid,mhjd->mhij", ssd_grad, scaled_x)).astype(f32)
    damped = weights_grad * decays
    coupling_low = to_low(jnp.sum(damped, axis=1))
    spread = damped * coupling[:, None]
    cumul_grad = jnp.sum(spread, axis=3) - jnp.sum(spread, axis=2)
    out_state_grad = to_low(batched("mij,mjs->mis", coupling_low, state_in)).astype(f32)
    in_state_grad = to_low(batched("mij,mis->mjs", coupling_low, state_out)).astype(f32)
    scaled_grad = scaled_grad.transpose(0, 2, 1, 3).astype(f32)
    mixed_grad = ssm_y_grad * skip_gain[:, None] + scaled_grad * delta[..., None]
    rate_grad = jnp.einsum("ij,mhi->mjh", lower, cumul_grad, precision=lax.Precision.HIGHEST)
    delta_grad = jnp.sum(scaled_grad * mixed_x, axis=3) + rate_grad * rates
    decay_grad = jnp.sum(rate_grad * delta, axis=(0, 1)) * rates
    delta_in_grad = delta_grad * jax.nn.sigmoid(delta_raw + delta_bias)
    bias_grad = jnp.sum(delta_in_grad, axis=(0, 1))
    delta_raw_grad = to_low(delta_in_grad).reshape(total, SSM_HEADS)
    conv_out_grad = jnp.concatenate(
        [mixed_grad.reshape(micro, length, width), in_state_grad, out_state_grad], axis=2
    )
    conv_pre_grad = conv_out_grad * silu_slope(conv_pre)
    conv_bias_grad = jnp.sum(conv_pre_grad, axis=(0, 1))
    columns = [None] * KCONV
    columns[KCONV - 1] = jnp.sum(conv_pre_grad * conv_in, axis=(0, 1))
    conv_in_grad = conv_pre_grad * taps[:, KCONV - 1]
    for by in range(1, KCONV):
        masked = conv_pre_grad * masks[by - 1]
        columns[KCONV - 1 - by] = jnp.sum(masked * shift_down(conv_in, by), axis=(0, 1))
        conv_in_grad += shift_up(masked, by) * taps[:, KCONV - 1 - by]
    taps_grad = jnp.stack(columns, axis=1)

    attended_grad = to_low(right_product(mixer_grad, w_attn)).reshape(
        micro, length, KV_HEADS, group, HEAD_DIM
    )
    value_grad = to_low(batched("mgkij,migkd->mjgd", probs_low, attended_grad))
    prob_grad = batched("migkd,mjgd->mgkij", attended_grad, values)
    score_grad = to_low(probs * (prob_grad - jnp.sum(prob_grad * probs, axis=-1, keepdims=True)))
    query_grad = to_low(batched("mgkij,mjgd->migkd", score_grad, keys) * scale)
    key_grad = to_low(batched("mgkij,migkd->mjgd", score_grad, queries) * scale)

    joined = jnp.concatenate(
        [
            query_grad.reshape(total, q_width),
            key_grad.reshape(total, kv_width),
            value_grad.reshape(total, kv_width),
            gate_z_grad,
            to_low(conv_in_grad).reshape(total, chan),
            delta_raw_grad,
            jnp.zeros((total, tail_width - SSM_HEADS), jnp.bfloat16),
        ],
        axis=1,
    )
    normed_grad = to_low(right_product(joined, w_in)).astype(f32)
    input_part, gain1_grad = norm_backward(inputs, inverse1, gain1, normed_grad)
    input_grad = resid_grad + input_part
    grad_main = to_low(left_product(normed_low, joined[:, :main_width]))
    grad_delta = to_low(left_product(normed_low, delta_raw_grad))
    vector_grads = (gain1_grad, taps_grad, conv_bias_grad, gain3_grad, gain2_grad)
    flat = jnp.concatenate([to_low(grad).reshape(count, -1) for grad in vector_grads], axis=1)
    flat = jnp.pad(flat, ((0, 0), (0, small.size - flat.shape[1])))
    grad_in = jnp.concatenate(
        [
            grad_main,
            grad_delta,
            flat.reshape(model, small.shape[1]),
            jnp.zeros((model, spare), jnp.bfloat16),
        ],
        axis=1,
    )
    owned_in = lax.psum_scatter(grad_in, "dp", scatter_dimension=0, tiled=True).astype(f32)
    head_sums = lax.psum(jnp.concatenate([bias_grad, decay_grad, skip_grad]), "dp")

    bounds = [0, q_width, q_width + kv_width, q_width + 2 * kv_width]
    bounds += [bounds[-1] + width, bounds[-1] + 2 * width, main_width, main_width + SSM_HEADS]
    pieces = [owned_in[:, low:high] for low, high in zip(bounds[:-1], bounds[1:])]
    grad_query, grad_key, grad_value, grad_z, grad_x, grad_bc, grad_dt = pieces
    flat = owned_in[:, bounds[-1] : bounds[-1] + small.shape[1]].reshape(-1)
    owned = []
    offset = 0
    for vector in vectors:
        owned.append(flat[offset : offset + vector.size].reshape(vector.shape))
        offset += vector.size
    owned_mix = owned_mix.astype(f32)
    owned_ff = owned_ff.astype(f32)
    return (
        output.reshape(tokens.shape),
        input_grad.reshape(tokens.shape),
        owned[0],
        grad_query,
        grad_key,
        grad_value,
        owned_mix[:attn_rows],
        grad_z,
        grad_x,
        grad_bc,
        grad_dt,
        owned[1],
        owned[2],
        owned[3],
        owned_mix[attn_rows:],
        owned[4],
        owned_ff[:, :ff],
        owned_ff[:, ff:],
        owned_back.astype(f32),
        head_sums[:SSM_HEADS],
        head_sums[SSM_HEADS : 2 * SSM_HEADS],
        head_sums[2 * SSM_HEADS :],
    )


def solution(mesh):
    placed = (
        P(None, "dp", None),
        P(None, "dp", None),
        P(None, "dp", None),
        P("dp"),
        P("dp", None),
        P("dp", None),
        P("dp", None),
        P("dp", None),
        P("dp", None),
        P("dp", None),
        P("dp", None),
        P("dp", None),
        P("dp", None),
        P("dp"),
        P("dp"),
        P("dp", None),
        P("dp"),
        P("dp", None),
        P("dp", None),
        P("dp", None),
        P(),
        P(),
        P(),
    )
    return jax.shard_map(
        per_device,
        mesh=mesh,
        in_specs=placed,
        out_specs=(
            P(None, "dp", None),
            P(None, "dp", None),
            P("dp"),
            P("dp", None),
            P("dp", None),
            P("dp", None),
            P("dp", None),
            P("dp", None),
            P("dp", None),
            P("dp", None),
            P("dp", None),
            P("dp", None),
            P("dp"),
            P("dp"),
            P("dp", None),
            P("dp"),
            P("dp", None),
            P("dp", None),
            P("dp", None),
            P(),
            P(),
            P(),
        ),
        check_vma=False,
    )
```
